32 devices in a mesh: dp: 16 (over z, y, core), shard: 2 (over x).
Axes of the slice: x: 2, y: 2, z: 4, core: 2. Of those that a mesh axis runs over, the one named last changes fastest.
Arguments:
- inputs: bfloat16 [16384, 1600], P(('dp', 'shard')), may hold values from -6 to 6
- cotangent: bfloat16 [16384, 1600], P(('dp', 'shard')), may hold values from -6 to 6
- seq_lengths: int32 [32, 4], P(('dp', 'shard')), may hold values from 0 to 512, as said below
- qkv_weight: float32 [1600, 4800], P('shard'), may hold values from -0.15625 to 0.15625
- out_weight: float32 [1600, 1600], P('shard'), may hold values from -0.625 to 0.625
- up_weight: float32 [1600, 6400], P('shard'), may hold values from -0.15625 to 0.15625
- down_weight: float32 [6400, 1600], P('shard'), may hold values from -0.078125 to 0.078125
- vector_params: float32 [19200], P('shard'), may hold values from -0.6 to 1.45, as said below
- qkv_momentum: float32 [1600, 4800], P('shard'), may hold values from -16 to 16
- out_momentum: float32 [1600, 1600], P('shard'), may hold values from -6 to 6
- up_momentum: float32 [1600, 6400], P('shard'), may hold values from -40 to 40
- down_momentum: float32 [6400, 1600], P('shard'), may hold values from -40 to 40
- vector_momentum: float32 [19200], P('shard'), may hold values from -64 to 64
- qkv_variance: float32 [1600, 4800], P('shard'), may hold values from 0.32768 to 2.62144
- out_variance: float32 [1600, 1600], P('shard'), may hold values from 0.1851392 to 1.47456
- up_variance: float32 [1600, 6400], P('shard'), may hold values from 2.048 to 16.384
- down_variance: float32 [6400, 1600], P('shard'), may hold values from 2.048 to 16.384
- vector_variance: float32 [19200], P('shard'), may hold values from 5.24288 to 41.94304
Outputs:
- layer_output: bfloat16 [16384, 1600], P(('dp', 'shard'))
- input_grad: bfloat16 [16384, 1600], P(('dp', 'shard'))
- updated_qkv: float32 [1600, 4800], P('shard')
- updated_out: float32 [1600, 1600], P('shard')
- updated_up: float32 [1600, 6400], P('shard')
- updated_down: float32 [6400, 1600], P('shard')
- updated_vector: float32 [19200], P('shard')
- momentum_qkv: float32 [1600, 4800], P('shard')
- momentum_out: float32 [1600, 1600], P('shard')
- momentum_up: float32 [1600, 6400], P('shard')
- momentum_down: float32 [6400, 1600], P('shard')
- momentum_vector: float32 [19200], P('shard')
- variance_qkv: float32 [1600, 4800], P('shard')
- variance_out: float32 [1600, 1600], P('shard')
- variance_up: float32 [1600, 6400], P('shard')
- variance_down: float32 [6400, 1600], P('shard')
- variance_vector: float32 [19200], P('shard')
The draws below stay inside these ranges and needn't reach their ends.
Inputs may be any that keep to these rules, and one draw needn't show every extreme that they name: `seq_lengths`: on each device the blocks that its sequences take, ceil(length / 128) each, add up to at most 4. A zero is an empty entry. Some device holds a sequence of 512 tokens. `vector_params`: entries of the two gains lie near one, those of the biases near zero.
All inputs are finite; a program needn't handle non-finite values.
Results may differ from the reference program's by a relative error of at most 0.012.
The reference program's roundings to bfloat16 on the way count: a program that leaves them out, or rounds other values in their place, can miss the bound.
Values may be sent and summed in bfloat16 or wider, within the bound.
No kernel may reach another device: no remote copies, remote signals or barrier semaphores. Data moves between devices by JAX's collectives and lax.ppermute only.
A program may use at most 832 MiB of HBM per device.

```python
import math
import jax
import jax.numpy as jnp
from jax import lax

D = 1600
FF = 6400
HD = 64
SLOTS = 512
BLK = 128
SEQ_DEV = 4
STEP = 10
LMAX = 512
TOKENS = 16384
VEC = 19200
N_DP = 16
N_SHARD = 2


def draw_seq_lengths(key, part):
    key = jax.random.fold_in(key, 11)
    devices = N_DP * N_SHARD
    total_blocks = SLOTS // BLK
    most_blocks = LMAX // BLK
    key_used, key_cuts, key_trim, key_chosen = jax.random.split(key, 4)
    blocks_used = jax.random.randint(key_used, (devices, 1), total_blocks // 2, total_blocks + 1)
    cut_points = jnp.sort(jax.random.randint(key_cuts, (devices, SEQ_DEV - 1), 0, blocks_used + 1), axis=1)
    cut_edges = jnp.concatenate([jnp.zeros((devices, 1), jnp.int32), cut_points, blocks_used], axis=1)
    pieces = jnp.minimum(cut_edges[:, 1:] - cut_edges[:, :-1], most_blocks)
    trimmed = jax.random.randint(key_trim, (devices, SEQ_DEV), 0, BLK)
    lengths_out = jnp.where(pieces > 0, pieces * BLK - trimmed, 0)
    chosen = jax.random.randint(key_chosen, (), 0, devices)
    long_row = jnp.where(jnp.arange(SEQ_DEV) == 0, LMAX, 0)
    lengths_out = jnp.where(jnp.arange(devices)[:, None] == chosen, long_row[None, :], lengths_out)
    return lengths_out.astype(jnp.int32)


def draw_vector_params(key, part):
    key = jax.random.fold_in(key, 5)
    places = jnp.arange(8 * D + FF)
    is_gain = (places < D) | (places >= 5 * D) & (places < 6 * D)
    normal_draw = jnp.clip(jax.random.normal(key, (8 * D + FF,), jnp.float32), -3.0, 3.0)
    return jnp.where(is_gain, 1.0 + 0.15 * normal_draw, 0.2 * normal_draw).astype(jnp.float32)


def steps_of(stream_key, shape, shards, least, top_value):
    loudness = 1.0
    for dim, shards_of in shards:
        heights = jax.random.uniform(jax.random.fold_in(jax.random.fold_in(stream_key, 6), dim), (shards_of,), jnp.float32, least / len(shards), top_value / len(shards))
        loudness = loudness * jnp.repeat(jnp.exp(heights), shape[dim] // shards_of).reshape((-1,) + (1,) * (len(shape) - 1 - dim))
    return loudness


def bell_draw(rng, dims, scale, bound, shards=(), kind=jnp.bfloat16):
    drawn = jax.random.normal(rng, dims, jnp.float32) * scale
    if len(shards) > 0:
        drawn = steps_of(rng, dims, shards, -0.22, 0.18) * drawn
    return jnp.clip(drawn, min=-bound, max=bound).astype(kind)


def setup_inputs(seed: int = 0) -> dict:
    arg_keys = jax.random.split(jax.random.key(seed), 19)
    inputs = bell_draw(arg_keys[0], (TOKENS, D), 1.0, 6.0, ((0, 32),))
    cotangent = bell_draw(arg_keys[1], (TOKENS, D), 1.0, 6.0, ((0, 32),))
    seq_lengths = draw_seq_lengths(jax.random.fold_in(arg_keys[18], 71), 0)
    qkv_weight = bell_draw(arg_keys[3], (D, 3 * D), D ** -0.5, 0.15625, ((0, 2),), jnp.float32)
    out_weight = bell_draw(arg_keys[4], (D, D), (D // 16) ** -0.5, 0.625, ((0, 2),), jnp.float32)
    up_weight = bell_draw(arg_keys[5], (D, FF), D ** -0.5, 0.15625, ((0, 2),), jnp.float32)
    down_weight = bell_draw(arg_keys[6], (FF, D), FF ** -0.5, 0.078125, ((0, 2),), jnp.float32)
    vector_params = draw_vector_params(jax.random.fold_in(arg_keys[18], 71), 0)
    qkv_momentum = bell_draw(arg_keys[8], (D, 3 * D), (0.022 * TOKENS ** 0.5), 16.0, ((0, 2),), jnp.float32)
    out_momentum = bell_draw(arg_keys[9], (D, D), (0.017 * TOKENS ** 0.5), 6.0, ((0, 2),), jnp.float32)
    up_momentum = bell_draw(arg_keys[10], (D, FF), (0.055 * TOKENS ** 0.5), 40.0, ((0, 2),), jnp.float32)
    down_momentum = bell_draw(arg_keys[11], (FF, D), (0.055 * TOKENS ** 0.5), 40.0, ((0, 2),), jnp.float32)
    vector_momentum = bell_draw(arg_keys[12], (VEC,), (0.089 * TOKENS ** 0.5), 64.0, ((0, 2),), jnp.float32)
    qkv_variance = jnp.clip(jnp.exp(math.log(2.62144) - 2.0794415 * jax.random.uniform(arg_keys[13], (D, 3 * D), jnp.float32) ** steps_of(arg_keys[13], (D, 3 * D), ((0, 2),), -0.2, 0.2)), 0.32768, 2.62144)
    out_variance = jnp.clip(jnp.exp(math.log(1.47456) - 2.075007 * jax.random.uniform(arg_keys[14], (D, D), jnp.float32) ** steps_of(arg_keys[14], (D, D), ((0, 2),), -0.2, 0.2)), 0.1851392, 1.47456)
    up_variance = jnp.clip(jnp.exp(math.log(16.384) - 2.0794415 * jax.random.uniform(arg_keys[15], (D, FF), jnp.float32) ** steps_of(arg_keys[15], (D, FF), ((0, 2),), -0.2, 0.2)), 2.048, 16.384)
    down_variance = jnp.clip(jnp.exp(math.log(16.384) - 2.0794415 * jax.random.uniform(arg_keys[16], (FF, D), jnp.float32) ** steps_of(arg_keys[16], (FF, D), ((0, 2),), -0.2, 0.2)), 2.048, 16.384)
    vector_variance = jnp.clip(jnp.exp(math.log(41.94304) - 2.0794415 * jax.random.uniform(arg_keys[17], (VEC,), jnp.float32) ** steps_of(arg_keys[17], (VEC,), ((0, 2),), -0.2, 0.2)), 5.24288, 41.94304)
    return dict(inputs=inputs, cotangent=cotangent, seq_lengths=seq_lengths, qkv_weight=qkv_weight, out_weight=out_weight, up_weight=up_weight, down_weight=down_weight, vector_params=vector_params, qkv_momentum=qkv_momentum, out_momentum=out_momentum, up_momentum=up_momentum, down_momentum=down_momentum, vector_momentum=vector_momentum, qkv_variance=qkv_variance, out_variance=out_variance, up_variance=up_variance, down_variance=down_variance, vector_variance=vector_variance)


@jax.custom_vjp
def low(v):
    return lax.optimization_barrier(v.astype(jnp.bfloat16)).astype(jnp.float32)

@jax.custom_vjp
def low_back(v):
    return v

def low_keep(v):
    return (low(v), None)

def low_pass(kept, grad):
    return (grad,)

def back_keep(v):
    return (v, None)

def back_low(kept, grad):
    return (low(grad),)
low.defvjp(low_keep, low_pass)
low_back.defvjp(back_keep, back_low)
NEG_FILL = -1e+30
NORM_EPS = 1e-05
GELU_SCALE = 0.7978845608028654
BETA_ONE = 0.9
BETA_TWO = 0.999
LEARN_RATE = 0.06
VECTOR_RATE = 0.25
ADAM_EPS = 1e-08
WEIGHT_DECAY = 0.1

def layer_norm(values, gain_vec, shift_vec):
    center = values - lax.optimization_barrier(jnp.mean(values, axis=-1, keepdims=True))
    spread = lax.optimization_barrier(jnp.mean(center * center, axis=-1, keepdims=True))
    return center * lax.rsqrt(spread + NORM_EPS) * gain_vec + shift_vec

def gelu_tanh(values):
    return 0.5 * values * (1.0 + jnp.tanh(GELU_SCALE * (values + 0.044715 * values * values * values)))

def layout(row_lengths, slot_count, block_size):
    blocks_used = ((row_lengths + block_size - 1) // block_size).astype(jnp.int32)
    starts = ((jnp.cumsum(blocks_used).astype(jnp.int32) - blocks_used) * block_size).astype(jnp.int32)
    position = jnp.arange(slot_count, dtype=jnp.int32)[:, None]
    inside = (position >= starts[None, :]) & (position < (starts + row_lengths)[None, :])
    labels = jnp.arange(row_lengths.shape[0], dtype=jnp.int32) + 1
    segment = lax.optimization_barrier(jnp.sum(jnp.where(inside, labels[None, :], 0), axis=1)).astype(jnp.int32) - 1
    return segment.astype(jnp.int32)

def split_vector(vector, model_width, hidden):
    pieces = [vector[number * model_width:(number + 1) * model_width] for number in range(7)]
    bias_up = vector[7 * model_width:7 * model_width + hidden]
    bias_down = vector[7 * model_width + hidden:]
    return pieces + [bias_up, bias_down]

def block_forward(qkv_w, out_w, up_w, down_w, vector, token_rows, segment):
    slot_count, model_width = token_rows.shape
    hidden = up_w.shape[1]
    head_count = model_width // HD
    gain_one, shift_one, bias_query, bias_value, bias_out, gain_two, shift_two, bias_up, bias_down = split_vector(vector, model_width, hidden)
    normed = low(layer_norm(token_rows, gain_one, shift_one))
    qkv_bias = jnp.concatenate([bias_query, jnp.zeros((model_width,), jnp.float32), bias_value])
    projected = low(low_back(jnp.dot(normed, qkv_w, precision=lax.Precision.HIGHEST) + qkv_bias))
    queries = projected[:, :model_width].reshape(slot_count, head_count, HD)
    key_heads = projected[:, model_width:2 * model_width].reshape(slot_count, head_count, HD)
    values = projected[:, 2 * model_width:].reshape(slot_count, head_count, HD)
    scores = low_back(jnp.einsum('qhd,khd->hqk', queries, key_heads, precision=lax.Precision.HIGHEST) * 0.125)
    position = jnp.arange(slot_count, dtype=jnp.int32)
    allowed = (segment[:, None] == segment[None, :]) & (position[None, :] <= position[:, None])
    scores = jnp.where(allowed[None], scores, NEG_FILL)
    row_max = lax.optimization_barrier(jnp.max(scores, axis=-1, keepdims=True))
    exponent = jnp.exp(scores - row_max)
    attn_probs = low(exponent / lax.optimization_barrier(jnp.sum(exponent, axis=-1, keepdims=True)))
    attended = jnp.einsum('hqk,khd->qhd', attn_probs, values, precision=lax.Precision.HIGHEST).reshape(slot_count, model_width)
    attended = low(low_back(attended))
    residual = token_rows + low_back(jnp.dot(attended, out_w, precision=lax.Precision.HIGHEST) + bias_out)
    normed_two = low(layer_norm(residual, gain_two, shift_two))
    pre_act = low_back(jnp.dot(normed_two, up_w, precision=lax.Precision.HIGHEST) + bias_up)
    activated = low(gelu_tanh(pre_act))
    return residual + low_back(jnp.dot(activated, down_w, precision=lax.Precision.HIGHEST) + bias_down)

def adamw_step(master, gradient, momentum, variance, decay_rate, step_rate):
    momentum_new = BETA_ONE * momentum + (1.0 - BETA_ONE) * gradient
    variance_new = BETA_TWO * variance + (1.0 - BETA_TWO) * gradient * gradient
    corrected_m = momentum_new / (1.0 - BETA_ONE ** STEP)
    corrected_v = variance_new / (1.0 - BETA_TWO ** STEP)
    updated = master - step_rate * (corrected_m / (jnp.sqrt(corrected_v) + ADAM_EPS) + decay_rate * master)
    return (updated, momentum_new, variance_new)

def reference(inputs, cotangent, seq_lengths, qkv_weight, out_weight, up_weight, down_weight, vector_params, qkv_momentum, out_momentum, up_momentum, down_momentum, vector_momentum, qkv_variance, out_variance, up_variance, down_variance, vector_variance):
    devices = seq_lengths.shape[0]
    slot_count = inputs.shape[0] // devices
    model_width = inputs.shape[1]
    segments = jax.vmap(lambda row_lengths: layout(row_lengths, slot_count, BLK))(seq_lengths)
    live_rows = (segments >= 0)[..., None]
    token_rows = inputs.astype(jnp.float32).reshape(devices, slot_count, model_width)
    grad_rows = jnp.where(live_rows, cotangent.astype(jnp.float32).reshape(devices, slot_count, model_width), 0.0)
    device_step = jax.checkpoint(block_forward)

    def forward(qkv_w, out_w, up_w, down_w, vector, all_rows):
        working = (low(qkv_w), low(out_w), low(up_w), low(down_w), low(vector))

        def scan_body(running, block_item):
            return (running, device_step(working[0], working[1], working[2], working[3], working[4], block_item[0], block_item[1]))
        _, outputs = lax.scan(scan_body, jnp.zeros((), jnp.float32), (all_rows, segments))
        return outputs
    outputs, pullback = jax.vjp(forward, qkv_weight, out_weight, up_weight, down_weight, vector_params, token_rows)
    gradients = pullback(grad_rows)
    layer_output = jnp.where(live_rows, outputs, 0.0).reshape(-1, model_width).astype(jnp.bfloat16)
    input_grad = gradients[5].reshape(-1, model_width).astype(jnp.bfloat16)
    new_qkv = adamw_step(qkv_weight, gradients[0], qkv_momentum, qkv_variance, WEIGHT_DECAY, LEARN_RATE)
    new_out = adamw_step(out_weight, gradients[1], out_momentum, out_variance, WEIGHT_DECAY, LEARN_RATE)
    new_up = adamw_step(up_weight, gradients[2], up_momentum, up_variance, WEIGHT_DECAY, LEARN_RATE)
    new_down = adamw_step(down_weight, gradients[3], down_momentum, down_variance, WEIGHT_DECAY, LEARN_RATE)
    new_vector = adamw_step(vector_params, gradients[4], vector_momentum, vector_variance, 0.0, VECTOR_RATE)
    return (layer_output, input_grad, new_qkv[0], new_out[0], new_up[0], new_down[0], new_vector[0], new_qkv[1], new_out[1], new_up[1], new_down[1], new_vector[1], new_qkv[2], new_out[2], new_up[2], new_down[2], new_vector[2])
```

```python
import functools

import jax
import jax.numpy as jnp
from jax import lax
from jax.experimental import pallas as pl
from jax.experimental.pallas import tpu as pltpu
from jax.sharding import PartitionSpec as P

HD = 64
BLK = 128
STEP = 10


NEG_FILL = -1e30
NORM_EPS = 1e-05
GELU_SCALE = 0.7978845608028654
GELU_CUBE = 0.044715
BETA_ONE = 0.9
BETA_TWO = 0.999
LEARN_RATE = 0.06
VECTOR_RATE = 0.25
ADAM_EPS = 1e-08
WEIGHT_DECAY = 0.1

BF16 = jnp.bfloat16
F32 = jnp.float32
VMEM_LIMIT = 44 * 1024 * 1024
TILE = 256
ISSUE = 1.0
LATENCY = 3.0
HOLD = 20.17
CAP = 5
ROWS = 256

NUDGES = (
    0, 0, -33.3, -4.1, -13.2, 3.2, -5.9, -16.2, 24, -9.4, 0.6, -6.3, 9.9, -2.6, -3, -2.6,
    0, 0, 4.4, -3.2, 19.6, -3.9, 18, 27.3, 0, 5.3, 21.8, -13.9, -12, 17.4, 0, -8.2,
    5.6, 0, 0.2, 11, 0, 0.8, -11, -0.3, 6.1, -13, 21.4, 18.2, 0, 29.5, -0.5, -34.4,
    19, 14.4, -0.3, -0.6, -7.6, 0, 6.8, 5.4, 39, 0, -8.4, -2.7, 4.5, 0, 34.6, 0,
    -7.2, 4.3, -2.5, -2, 0, -45.7, -22.9, 10.9, 0, -1, -5.3, 0, -19.9, 14.6, -28.3, -19.2,
    -18.1, 0, -3.6, 7.5, 54.8, 6, -51.4, -26.3, -4.4, 20, 7.5, 0, 0, 0, 2.3, 0.7,
    -0.8, -1.2, 3.3, 4.6, 5.1, 0, 6.8, 19.6, -6.2, 8.6, 30.8, -28.3, -21.1, -2.1, 1.3, -36.9,
    -14, -2.4, 0, -0.3, 2.5, -0.9, 2.1, 0, 5.6, -3.9, -11.7, 6.9, 2.5, 54.5, 17.9, -1.2,
    -15, -25.2, 0.2, 0, 28.8, 6.2, -21.8, 0,
)

AXES = ("dp", "shard")
BIT_HALF = 1
BIT_CORE = 2
BIT_Y = 4
BIT_Z = 8
BIT_REST = 16


class Task:
    def __init__(self, name, kind, rank, cost, needs, run):
        self.name = name
        self.kind = kind
        self.rank = rank
        self.cost = cost
        self.needs = needs
        self.run = run
        self.value = None
        self.end = None


class Plan:
    def __init__(self):
        self.tasks = []

    def core(self, name, rank, cost, needs, run):
        task = Task(name, "core", rank, cost, needs, run)
        self.tasks.append(task)
        return task

    def link(self, name, rank, cost, needs, run):
        task = Task(name, "link", rank, cost, needs, run)
        self.tasks.append(task)
        return task

    def order(self):
        waiting = list(self.tasks)
        active = []
        flying = []
        steps = []
        now = 0.0

        def advance(until):
            nonlocal now
            while until is None or now < until:
                users = {}
                for task in active:
                    for axis, left in task.left.items():
                        if left > 1e-6:
                            users[axis] = users.get(axis, 0) + 1
                step = min(
                    [1e9 if until is None else until - now]
                    + [
                        left * users[axis]
                        for task in active
                        for axis, left in task.left.items()
                        if left > 1e-6
                    ]
                )
                now += step
                ended = False
                for task in list(active):
                    for axis, left in task.left.items():
                        if left > 1e-6:
                            task.left[axis] = left - step / users[axis]
                    if max(task.left.values()) <= 1e-6:
                        active.remove(task)
                        task.end = now
                        ended = True
                if until is None and ended:
                    return

        def done(task):
            return all(
                need.end is not None and need.end <= now and need not in flying
                for need in task.needs
            )

        while waiting:
            landed = [t for t in flying if t.end is not None and t.end + LATENCY <= now]
            for task in landed:
                flying.remove(task)
            queued = sorted((t for t in waiting if t.kind == "link" and done(t)), key=lambda t: t.rank)
            links = []
            for task in queued:
                if len(flying) == CAP or any(
                    sum(other.left.get(axis, 0.0) for other in active) > HOLD
                    for axis in task.cost
                    if axis != BIT_CORE
                ):
                    continue
                links.append(task)
                task.left = dict(task.cost)
                active.append(task)
                flying.append(task)
                waiting.remove(task)
                advance(now + ISSUE)
            cores = sorted((t for t in waiting if t.kind == "core" and done(t)), key=lambda t: t.rank)
            if cores:
                task = cores[0]
                waiting.remove(task)
                steps.append((landed, links, task))
                advance(now + task.cost)
                task.end = now
                continue
            if links or landed:
                steps.append((landed, links, None))
            if not any(t.end is not None for t in flying):
                advance(None)
            else:
                advance(now + 0.5)
        self.length = now
        return steps

    def trace(self):
        for task, nudge in zip(self.tasks, NUDGES):
            task.rank += nudge
        token = None
        for landed, links, task in self.order():
            group = links + ([task] if task is not None else [])
            arrived, token = lax.optimization_barrier(([t.value for t in landed], token))
            for member, value in zip(landed, arrived):
                member.value = value
            needed = [[need.value for need in member.needs] for member in group]
            needed, arrived, token = lax.optimization_barrier((needed, arrived, token))
            for member, value in zip(landed, arrived):
                member.value = value
            for member, values in zip(group, needed):
                with jax.named_scope(member.name):
                    member.value = member.run(*values)
            if task is not None:
                token = min(jax.tree.leaves(task.value), key=lambda leaf: leaf.size)


def layout(row_lengths, slot_count, block_size):
    blocks_used = (row_lengths + block_size - 1) // block_size
    starts = (jnp.cumsum(blocks_used) - blocks_used) * block_size
    position = jnp.arange(slot_count, dtype=jnp.int32)[:, None]
    inside = (position >= starts[None, :]) & (position < (starts + row_lengths)[None, :])
    labels = jnp.arange(row_lengths.shape[0], dtype=jnp.int32) + 1
    segment = jnp.sum(jnp.where(inside, labels[None, :], 0), axis=1) - 1
    return segment


def normalize(values):
    center = values - jnp.mean(values, axis=-1, keepdims=True)
    spread = jnp.mean(center * center, axis=-1, keepdims=True)
    inverse = lax.rsqrt(spread + NORM_EPS)
    return center * inverse, inverse


def normalize_back(grad, normal, inverse, gain_vec):
    scaled = grad * gain_vec
    mean_scaled = jnp.mean(scaled, axis=-1, keepdims=True)
    mean_cross = jnp.mean(scaled * normal, axis=-1, keepdims=True)
    return inverse * (scaled - mean_scaled - normal * mean_cross)


def column_sum(values):
    return jnp.sum(values, axis=0, keepdims=True)


def tiles(width, body, size=TILE):
    for start in range(0, width, size):
        body(slice(start, min(start + size, width)))


def dot_tile(x, w):
    return lax.dot_general(x, w, (((1,), (0,)), ((), ())), preferred_element_type=F32)


def dot_tile_t(x, w):
    return lax.dot_general(x, w, (((1,), (1,)), ((), ())), preferred_element_type=F32)


def params():
    return pltpu.CompilerParams(vmem_limit_bytes=VMEM_LIMIT)


def whole_block(shape):
    return pl.BlockSpec(shape, lambda *_: (0,) * len(shape))


def lead_block(shape, first=0):
    return pl.BlockSpec((1,) + shape, lambda j: (j + first,) + (0,) * len(shape))


def little():
    return pl.CostEstimate(flops=1, bytes_accessed=1, transcendentals=0)


class Weights:
    COUNT = 10

    def __init__(self, by_rows, spot, own, pieces):
        self.by_rows = by_rows
        self.operands = [spot, own] + list(pieces)
        self.width = own.shape[-1]

    def specs(self):
        return [pl.BlockSpec(memory_space=pltpu.SMEM)] + [pl.BlockSpec(memory_space=pl.ANY)] * 9

    def scratch(self):
        return [
            pltpu.VMEM((2, self.width, self.width), BF16),
            pltpu.SemaphoreType.DMA((2,)),
        ]


def start_block(by_rows, refs, buffer, sems, block, slot):
    spot, own, pieces = refs[0], refs[1], refs[2:]
    half, core, high, low = (spot[i] for i in range(4))
    width = buffer.shape[2]
    quarter = width // 4
    group, bit = block >> 1, block & 1

    def copy(source, start, size):
        rows = pl.ds(pl.multiple_of(start, 16), size)
        pltpu.make_async_copy(source, buffer.at[slot, rows], sems.at[slot]).start()

    if by_rows:
        copy(own.at[block], half * (2 * quarter), 2 * quarter)
        near = group == core
        for is_near in (True, False):
            outer, inner = (high, low) if is_near else (low, high)
            for flip in range(2):

                @pl.when((near == is_near) & ((bit ^ outer) == flip))
                def _(is_near=is_near, inner=inner, flip=flip):
                    for k in range(2):
                        start = ((1 - half) * 2 + (inner ^ k)) * quarter
                        copy(pieces[2 * (2 * flip + k) + (0 if is_near else 1)], start, quarter)

    else:

        @pl.when(group == half)
        def _():
            copy(own.at[bit], 0, width)

        for is_near in (True, False):
            outer, inner = (high, low) if is_near else (low, high)

            @pl.when((group != half) & ((bit == core) == is_near))
            def _(is_near=is_near, outer=outer, inner=inner):
                for flip in range(2):
                    for k in range(2):
                        start = ((outer ^ flip) * 2 + (inner ^ k)) * quarter
                        copy(pieces[2 * (2 * flip + k) + (0 if is_near else 1)], start, quarter)


def stream_block(by_rows, refs, buffer, sems, first):
    step = pl.program_id(0)
    slot = step & 1

    @pl.when(step == 0)
    def _():
        start_block(by_rows, refs, buffer, sems, step + first, slot)

    @pl.when(step + 1 < pl.num_programs(0))
    def _():
        start_block(by_rows, refs, buffer, sems, step + first + 1, 1 - slot)

    pltpu.make_async_copy(buffer.at[slot], buffer.at[slot], sems.at[slot]).wait()
    return slot


def norm_one_kernel(input_ref, gain_ref, shift_ref, normed_ref, rows_ref):
    for start in range(0, input_ref.shape[1], 128):
        part = slice(start, start + 128)
        rows = input_ref[:, part].astype(F32).T
        normal, _ = normalize(rows)
        normed_ref[part, :] = (normal * gain_ref[...] + shift_ref[...]).astype(BF16)
        rows_ref[part, :] = rows.astype(BF16)


def norm_one(inputs_t, gain, shift):
    width, rows = inputs_t.shape
    full = whole_block((rows, width))
    line = whole_block((1, width))
    shape = jax.ShapeDtypeStruct((rows, width), BF16)
    return pl.pallas_call(
        norm_one_kernel,
        in_specs=[whole_block((width, rows)), line, line],
        out_specs=[full, full],
        out_shape=[shape, shape],
        grid=(1,),
        compiler_params=params(),
        cost_estimate=little(),
        name="norm_one",
    )(inputs_t, gain, shift)


def mask_grad_kernel(grad_ref, live_ref, low_ref, sum_ref):
    sum_ref[...] = jnp.zeros_like(sum_ref)
    for start in range(0, grad_ref.shape[1], 128):
        part = slice(start, start + 128)
        rows = jnp.where(live_ref[:, part] > 0, grad_ref[:, part].astype(F32), 0.0).T
        low_ref[part, :] = rows.astype(BF16)
        sum_ref[...] += column_sum(rows)


def mask_grad(cotangent_t, live):
    width, rows = cotangent_t.shape
    return pl.pallas_call(
        mask_grad_kernel,
        in_specs=[whole_block((width, rows)), whole_block((1, rows))],
        out_specs=[whole_block((rows, width)), whole_block((1, width))],
        out_shape=[
            jax.ShapeDtypeStruct((rows, width), BF16),
            jax.ShapeDtypeStruct((1, width), F32),
        ],
        grid=(1,),
        compiler_params=params(),
        cost_estimate=little(),
        name="mask",
    )(cotangent_t, live)


def blocks_kernel(counts, *refs):
    ins = refs[: len(counts)]
    outs = refs[len(counts) :]
    number = 0
    for ref, count in zip(ins, counts):
        width = ref.shape[1] // count
        for j in range(count):
            outs[0][number] = ref[:, j * width : (j + 1) * width].astype(BF16)
            number += 1


def column_blocks(arrays, counts, step_rows):
    rows = arrays[0].shape[0]
    width = arrays[0].shape[1] // counts[0]
    blocks = sum(counts)
    return pl.pallas_call(
        functools.partial(blocks_kernel, counts),
        grid=(rows // step_rows,),
        in_specs=[pl.BlockSpec((step_rows, a.shape[1]), lambda i: (i, 0)) for a in arrays],
        out_specs=pl.BlockSpec((blocks, step_rows, width), lambda i: (0, i, 0)),
        out_shape=jax.ShapeDtypeStruct((blocks, rows, width), BF16),
        compiler_params=params(),
        cost_estimate=little(),
        name="cast",
    )(*arrays)


def weighted(kernel, weights, first, **call):
    inner = call.pop("operands")
    scratch = call.pop("scratch_shapes", [])
    specs = call.pop("in_specs")
    outs = call["out_shape"]
    out_count = len(outs) if isinstance(outs, list) else 1

    def body(*refs):
        weight_refs = refs[: Weights.COUNT]
        rest = refs[Weights.COUNT : Weights.COUNT + len(inner) + out_count]
        more = refs[Weights.COUNT + len(inner) + out_count :]
        buffer, sems = more[:2]
        slot = stream_block(weights.by_rows, weight_refs, buffer, sems, first)
        kernel(buffer, slot, *rest, *more[2:])

    return pl.pallas_call(
        body,
        in_specs=weights.specs() + specs,
        scratch_shapes=weights.scratch() + scratch,
        compiler_params=params(),
        cost_estimate=little(),
        **call,
    )(*weights.operands, *inner)


def project_kernel(w_ref, slot, x_ref, bias_ref, out_ref):
    def body(cols):
        total = dot_tile(x_ref[...], w_ref[slot, :, cols]) + bias_ref[0, :, cols]
        out_ref[0, :, cols] = total.astype(BF16)

    tiles(w_ref.shape[2], body, 512)


def project(normed, weights, bias):
    rows, width = normed.shape
    return weighted(
        project_kernel,
        weights,
        0,
        operands=[normed, bias],
        grid=(3,),
        in_specs=[whole_block((rows, width)), lead_block((1, width))],
        out_specs=lead_block((rows, width)),
        out_shape=jax.ShapeDtypeStruct((3, rows, width), BF16),
        name="project",
    )


def row_parts(rows, body):
    for start in range(0, rows, 128):
        body(slice(start, start + 128))


def out_kernel(
    w_ref, slot, x_ref, input_ref, bias_ref, gain_ref, shift_ref, residual_ref, normed_ref
):
    def body(cols):
        total = dot_tile(x_ref[...], w_ref[slot, :, cols]) + bias_ref[:, cols]
        residual_ref[:, cols] = input_ref[:, cols].astype(F32) + total

    tiles(w_ref.shape[2], body)

    def finish(part):
        normal, _ = normalize(residual_ref[part, :])
        normed_ref[part, :] = (normal * gain_ref[...] + shift_ref[...]).astype(BF16)

    row_parts(x_ref.shape[0], finish)


def out_and_norm(attended, weights, inputs, bias, gain, shift):
    rows, width = attended.shape
    full = whole_block((rows, width))
    line = whole_block((1, width))
    return weighted(
        out_kernel,
        weights,
        3,
        operands=[attended, inputs, bias, gain, shift],
        grid=(1,),
        in_specs=[full, full, line, line, line],
        out_specs=[full, full],
        out_shape=[
            jax.ShapeDtypeStruct((rows, width), F32),
            jax.ShapeDtypeStruct((rows, width), BF16),
        ],
        name="out",
    )


def up_kernel(w_ref, slot, x_ref, bias_ref, act_ref, slope_ref):
    def body(cols):
        pre = dot_tile(x_ref[...], w_ref[slot, :, cols]) + bias_ref[0, :, cols]
        square = pre * pre
        bend = jnp.tanh(GELU_SCALE * pre * (1.0 + GELU_CUBE * square))
        half = 0.5 + 0.5 * bend
        act_ref[0, :, cols] = (pre * half).astype(BF16)
        inner = GELU_SCALE + (3.0 * GELU_CUBE * GELU_SCALE) * square
        slope_ref[0, :, cols] = half + (0.5 * pre) * (1.0 - bend * bend) * inner

    tiles(w_ref.shape[2], body, 512)


def up_and_gelu(normed, weights, bias):
    rows, width = normed.shape
    return weighted(
        up_kernel,
        weights,
        0,
        operands=[normed, bias],
        grid=(4,),
        in_specs=[whole_block((rows, width)), lead_block((1, width))],
        out_specs=[lead_block((rows, width)), lead_block((rows, width))],
        out_shape=[
            jax.ShapeDtypeStruct((4, rows, width), BF16),
            jax.ShapeDtypeStruct((4, rows, width), F32),
        ],
        name="up",
    )


def grad_pre_kernel(w_ref, slot, x_ref, slope_ref, out_ref, sum_ref):
    def body(cols):
        total = dot_tile(x_ref[...], w_ref[slot, :, cols]) * slope_ref[0, :, cols]
        low = total.astype(BF16)
        out_ref[0, :, cols] = low
        sum_ref[0, :, cols] = column_sum(low.astype(F32))

    tiles(w_ref.shape[2], body)


def grad_pre_act(grad_low, weights, slope):
    rows, width = grad_low.shape
    return weighted(
        grad_pre_kernel,
        weights,
        0,
        operands=[grad_low, slope],
        grid=(4,),
        in_specs=[whole_block((rows, width)), lead_block((rows, width))],
        out_specs=[lead_block((rows, width)), lead_block((1, width))],
        out_shape=[
            jax.ShapeDtypeStruct((4, rows, width), BF16),
            jax.ShapeDtypeStruct((4, 1, width), F32),
        ],
        name="g_pre",
    )


def add_product_t(w_ref, slot, x_ref, total_ref, size=TILE):
    later = pl.program_id(0) > 0

    def body(cols):
        part = dot_tile_t(x_ref[0], w_ref[slot, cols, :])
        total_ref[:, cols] = jnp.where(later, total_ref[:, cols], 0.0) + part

    tiles(w_ref.shape[1], body, size)


def last_step():
    return pl.program_id(0) == pl.num_programs(0) - 1


def norm_two_back_kernel(
    w_ref, slot, x_ref, residual_ref, grad_ref, gain_ref, out_ref, low_ref, sums_ref, total_ref
):
    add_product_t(w_ref, slot, x_ref, total_ref, 512)

    @pl.when(last_step())
    def _():
        sums_ref[...] = jnp.zeros_like(sums_ref)

        def body(part):
            normal, inverse = normalize(residual_ref[part, :])
            grad = total_ref[part, :]
            back = normalize_back(grad, normal, inverse, gain_ref[...])
            back = grad_ref[part, :].astype(F32) + back
            low = back.astype(BF16)
            out_ref[part, :] = back
            low_ref[part, :] = low
            sums_ref[0:1, :] += column_sum(grad * normal)
            sums_ref[1:2, :] += column_sum(grad)
            sums_ref[2:3, :] += column_sum(low.astype(F32))

        row_parts(total_ref.shape[0], body)


def norm_two_back(grad_pre, weights, residual, grad_low, gain):
    blocks, rows, width = grad_pre.shape
    full = whole_block((rows, width))
    return weighted(
        norm_two_back_kernel,
        weights,
        0,
        operands=[grad_pre, residual, grad_low, gain],
        grid=(blocks,),
        in_specs=[lead_block((rows, width)), full, full, whole_block((1, width))],
        out_specs=[full, full, whole_block((8, width))],
        out_shape=[
            jax.ShapeDtypeStruct((rows, width), F32),
            jax.ShapeDtypeStruct((rows, width), BF16),
            jax.ShapeDtypeStruct((8, width), F32),
        ],
        scratch_shapes=[pltpu.VMEM((rows, width), F32)],
        name="n2_b",
    )


def norm_one_back_kernel(
    w_ref, slot, x_ref, input_ref, grad_ref, gain_ref, out_ref, sums_ref, total_ref
):
    add_product_t(w_ref, slot, x_ref, total_ref)

    @pl.when(last_step())
    def _():
        sums_ref[...] = jnp.zeros_like(sums_ref)

        def body(part):
            normal, inverse = normalize(input_ref[part, :].astype(F32))
            grad = total_ref[part, :]
            back = normalize_back(grad, normal, inverse, gain_ref[...])
            out_ref[:, part] = (grad_ref[part, :] + back).T.astype(BF16)
            sums_ref[0:1, :] += column_sum(grad * normal)
            sums_ref[1:2, :] += column_sum(grad)

        row_parts(total_ref.shape[0], body)


def norm_one_back(grad_parts, weights, inputs, grad_residual, gain):
    blocks, rows, width = grad_parts.shape
    full = whole_block((rows, width))
    return weighted(
        norm_one_back_kernel,
        weights,
        0,
        operands=[grad_parts, inputs, grad_residual, gain],
        grid=(blocks,),
        in_specs=[lead_block((rows, width)), full, full, whole_block((1, width))],
        out_specs=[whole_block((width, rows)), whole_block((8, width))],
        out_shape=[
            jax.ShapeDtypeStruct((width, rows), BF16),
            jax.ShapeDtypeStruct((8, width), F32),
        ],
        scratch_shapes=[pltpu.VMEM((rows, width), F32)],
        name="n1_b",
    )


def layer_out_kernel(w_ref, slot, x_ref, residual_ref, live_ref, bias_ref, out_ref, total_ref):
    add_product_t(w_ref, slot, x_ref, total_ref, 1600)

    @pl.when(last_step())
    def _():
        def body(part):
            result = residual_ref[part, :] + (total_ref[part, :] + bias_ref[...])
            out_ref[:, part] = jnp.where(live_ref[:, part] > 0, result.T, 0.0).astype(BF16)

        row_parts(total_ref.shape[0], body)


def layer_out(activated, weights, residual, live, bias):
    blocks, rows, width = activated.shape
    full = whole_block((rows, width))
    return weighted(
        layer_out_kernel,
        weights,
        0,
        operands=[activated, residual, live, bias],
        grid=(blocks,),
        in_specs=[
            lead_block((rows, width)),
            full,
            whole_block((1, rows)),
            whole_block((1, width)),
        ],
        out_specs=whole_block((width, rows)),
        out_shape=jax.ShapeDtypeStruct((width, rows), BF16),
        scratch_shapes=[pltpu.VMEM((rows, width), F32)],
        name="layer",
    )


def grad_attended_kernel(w_ref, slot, x_ref, out_ref):
    def body(cols):
        out_ref[:, cols] = dot_tile_t(x_ref[...], w_ref[slot, cols, :]).astype(BF16)

    tiles(w_ref.shape[1], body)


def grad_attended_of(grad_branch, weights):
    rows, width = grad_branch.shape
    full = whole_block((rows, width))
    return weighted(
        grad_attended_kernel,
        weights,
        3,
        operands=[grad_branch],
        grid=(1,),
        in_specs=[full],
        out_specs=full,
        out_shape=jax.ShapeDtypeStruct((rows, width), BF16),
        name="g_att",
    )


def outer_kernel(extra, places_ref, left_ref, right_ref, *refs):
    total = lax.dot_general(
        left_ref[0], right_ref[0], (((0,), (0,)), ((), ())), preferred_element_type=F32
    )
    if extra:
        total = total + refs[0][0].astype(F32)
    refs[-1][0] = total.astype(BF16)


def outer_products(left, right, places, other=None):
    _, rows, width = left.shape
    count = places.shape[0] // 2
    part = pl.BlockSpec((1, TILE, width), lambda b, i, at: (b, i, 0))
    extra = [] if other is None else [other]
    return pl.pallas_call(
        functools.partial(outer_kernel, bool(extra)),
        grid_spec=pltpu.PrefetchScalarGridSpec(
            num_scalar_prefetch=1,
            grid=(count, pl.cdiv(width, TILE)),
            in_specs=[
                pl.BlockSpec((1, rows, TILE), lambda b, i, at: (at[2 * b], 0, i)),
                pl.BlockSpec((1, rows, width), lambda b, i, at: (at[2 * b + 1], 0, 0)),
            ]
            + [part] * len(extra),
            out_specs=part,
        ),
        out_shape=jax.ShapeDtypeStruct((count, width, width), BF16),
        compiler_params=params(),
        cost_estimate=little(),
        name="outer",
    )(places, left, right, *extra)


def head_lanes(ref, index, head, valid, lane):
    mine = valid & ((lane < HD) if head == 0 else (lane >= HD))
    return jnp.where(mine, ref[index], jnp.zeros((), BF16))


def attend_kernel(width, qkv_ref, fill_ref, out_ref, lse_ref):
    pair = pl.program_id(0)
    rows = qkv_ref.shape[1]
    lane = lax.broadcasted_iota(jnp.int32, (rows, 2 * HD), 1)
    valid = lane + pair * (2 * HD) < width
    totals = [None] * (rows // ROWS)
    column = lax.broadcasted_iota(jnp.int32, (ROWS, lse_ref.shape[1]), 1)
    for head in range(2):
        query = head_lanes(qkv_ref, 0, head, valid, lane) * 0.125
        key = head_lanes(qkv_ref, 1, head, valid, lane)
        value = head_lanes(qkv_ref, 2, head, valid, lane)
        for number in range(rows // ROWS):
            part = slice(number * ROWS, (number + 1) * ROWS)
            seen = slice(0, (number + 1) * ROWS)
            scores = dot_tile_t(query[part], key[seen]) + fill_ref[part, seen]
            row_max = jnp.max(scores, axis=-1, keepdims=True)
            exponent = jnp.exp(scores - row_max)
            total = jnp.sum(exponent, axis=-1, keepdims=True)
            probs = (exponent * (1.0 / total)).astype(BF16)
            result = dot_tile(probs, value[seen])
            totals[number] = result if head == 0 else totals[number] + result
            lse = row_max + jnp.log(total)
            lse_ref[part, :] = jnp.where(column == pair * 2 + head, lse, lse_ref[part, :])
    for number in range(rows // ROWS):
        out_ref[number * ROWS : (number + 1) * ROWS, :] = totals[number].astype(BF16)


def attend_forward(projected, fill):
    _, rows, width = projected.shape
    pairs = pl.cdiv(width, 2 * HD)
    return pl.pallas_call(
        functools.partial(attend_kernel, width),
        grid=(pairs,),
        in_specs=[
            pl.BlockSpec((3, rows, 2 * HD), lambda h: (0, 0, h)),
            whole_block((rows, rows)),
        ],
        out_specs=[
            pl.BlockSpec((rows, 2 * HD), lambda h: (0, h)),
            whole_block((rows, 128)),
        ],
        out_shape=[
            jax.ShapeDtypeStruct((rows, width), BF16),
            jax.ShapeDtypeStruct((rows, 128), F32),
        ],
        compiler_params=params(),
        cost_estimate=little(),
        name="attend",
    )(projected, fill)


def attend_back_kernel(width, first, qkv_ref, grad_ref, fill_ref, lse_ref, *refs):
    out_ref, query_ref, key_ref, value_ref = refs[-4:]
    pair = pl.program_id(0) + first
    rows = qkv_ref.shape[1]
    lane = lax.broadcasted_iota(jnp.int32, (rows, 2 * HD), 1)
    valid = lane + pair * (2 * HD) < width
    column = lax.broadcasted_iota(jnp.int32, (ROWS, lse_ref.shape[1]), 1)
    query_ref[...] = jnp.zeros_like(query_ref)
    key_ref[...] = jnp.zeros_like(key_ref)
    value_ref[...] = jnp.zeros_like(value_ref)
    contract = (((0,), (0,)), ((), ()))
    for head in range(2):
        query = head_lanes(qkv_ref, 0, head, valid, lane) * 0.125
        key = head_lanes(qkv_ref, 1, head, valid, lane)
        value = head_lanes(qkv_ref, 2, head, valid, lane)
        grad_mine = valid & ((lane < HD) if head == 0 else (lane >= HD))
        grad = jnp.where(grad_mine, grad_ref[...], jnp.zeros((), BF16))
        for number in range(rows // ROWS):
            part = slice(number * ROWS, (number + 1) * ROWS)
            seen = slice(0, (number + 1) * ROWS)
            lse = jnp.sum(
                jnp.where(column == pair * 2 + head, lse_ref[part, :], 0.0), axis=-1, keepdims=True
            )
            scores = dot_tile_t(query[part], key[seen]) + fill_ref[part, seen]
            probs = jnp.exp(scores - lse)
            grad_probs = dot_tile_t(grad[part], value[seen])
            inner = jnp.sum(grad_probs * probs, axis=-1, keepdims=True)
            grad_scores = (probs * (grad_probs - inner)).astype(BF16)
            query_ref[part, :] += dot_tile(grad_scores, key[seen])
            key_ref[seen, :] += lax.dot_general(
                grad_scores, query[part], contract, preferred_element_type=F32
            )
            value_ref[seen, :] += lax.dot_general(
                probs.astype(BF16), grad[part], contract, preferred_element_type=F32
            )
    out_ref[0] = (query_ref[...] * 0.125).astype(BF16)
    out_ref[1] = key_ref[...].astype(BF16)
    out_ref[2] = value_ref[...].astype(BF16)


def attend_backward(projected, grad_attended, fill, lse, first, count, earlier=None):
    _, rows, width = projected.shape
    three = pl.BlockSpec((3, rows, 2 * HD), lambda h: (0, 0, h + first))
    kept = [] if earlier is None else [earlier]
    return pl.pallas_call(
        functools.partial(attend_back_kernel, width, first),
        grid=(count,),
        in_specs=[
            three,
            pl.BlockSpec((rows, 2 * HD), lambda h: (0, h + first)),
            whole_block((rows, rows)),
            whole_block((rows, 128)),
        ]
        + [pl.BlockSpec(memory_space=pl.ANY)] * len(kept),
        out_specs=three,
        out_shape=jax.ShapeDtypeStruct((3, rows, width), BF16),
        scratch_shapes=[pltpu.VMEM((rows, 2 * HD), F32)] * 3,
        input_output_aliases={4: 0} if kept else {},
        compiler_params=params(),
        cost_estimate=little(),
        name="attend_b",
    )(projected, grad_attended, fill, lse, *kept)


def adamw_step(master, gradient, momentum, variance, decay_rate, step_rate):
    momentum_new = BETA_ONE * momentum + (1.0 - BETA_ONE) * gradient
    variance_new = BETA_TWO * variance + (1.0 - BETA_TWO) * gradient * gradient
    corrected_m = momentum_new / (1.0 - BETA_ONE**STEP)
    corrected_v = variance_new / (1.0 - BETA_TWO**STEP)
    updated = master - step_rate * (
        corrected_m / (jnp.sqrt(corrected_v) + ADAM_EPS) + decay_rate * master
    )
    return (updated, momentum_new, variance_new)


def adamw_kernel(picks, core_ref, w_ref, m_ref, v_ref, *refs):
    nw_ref, nm_ref, nv_ref = refs[-3:]
    first = core_ref[0] == 0
    blocks = []
    for number, core in picks:
        own, other = (refs[2 * number + i][0].astype(F32) for i in range(2))
        blocks.append(jnp.where(first, own, other) if core == 0 else jnp.where(first, other, own))
    gradient = blocks[0] if len(blocks) == 1 else jnp.concatenate(blocks, axis=1)
    nw_ref[...], nm_ref[...], nv_ref[...] = adamw_step(
        w_ref[...], gradient, m_ref[...], v_ref[...], WEIGHT_DECAY, LEARN_RATE
    )


def adamw_part(core, state, picks, step_rows, row_part=0, col_part=0, earlier=None):
    _, rows, width = picks[0][0][0].shape
    cols = len(picks) * width
    steps = rows // step_rows
    spec = pl.BlockSpec((step_rows, cols), lambda i: (i + row_part * steps, col_part))
    flat, grad_specs, chosen, known = [], [], [], []
    for pair, entry, from_core in picks:
        if (id(pair), entry) not in known:
            known.append((id(pair), entry))
            flat += list(pair)
            grad_specs += [
                pl.BlockSpec((1, step_rows, width), lambda i, entry=entry: (entry, i, 0))
            ] * 2
        chosen.append((known.index((id(pair), entry)), from_core))
    kept = [] if earlier is None else list(earlier)
    shape = jax.ShapeDtypeStruct(state[0].shape, F32)
    return pl.pallas_call(
        functools.partial(adamw_kernel, chosen),
        grid=(steps,),
        in_specs=[pl.BlockSpec(memory_space=pltpu.SMEM)]
        + [spec] * 3
        + grad_specs
        + [pl.BlockSpec(memory_space=pl.ANY)] * len(kept),
        out_specs=[spec] * 3,
        out_shape=[shape] * 3,
        input_output_aliases={4 + len(flat) + i: i for i in range(len(kept))},
        compiler_params=params(),
        cost_estimate=little(),
        name="adamw",
    )(core, *state, *flat, *kept)


def pick(array, index, axis=0):
    return lax.dynamic_index_in_dim(array, index, axis, keepdims=False)


def add_low(*terms):
    total = terms[0].astype(F32)
    for term in terms[1:]:
        total = total + term.astype(F32)
    return total.astype(BF16)


class Links:
    def __init__(self, plan, devices):
        self.plan = plan
        self.devices = devices
        self.half = lax.axis_index("shard")
        index = lax.axis_index("dp")
        self.core = index % 2
        self.y = (index // 2) % 2
        self.z = (index // 4) % 2

    def swap(self, name, rank, needs, prepare, size, bit, bit_one=None):
        bit_one = bit if bit_one is None else bit_one
        pairs = [(i, i ^ (bit_one if i & BIT_CORE else bit)) for i in range(self.devices)]
        cost = {}
        for each in (bit, bit_one):
            rate = 6e5 if each == BIT_CORE else 1e5
            hops = 2 if each >= BIT_REST else 1
            share = 0.5 if each == BIT_CORE else 1.0
            cost[each] = cost.get(each, 0.0) + size * 2.08 * hops * share / rate

        def run(*values):
            return lax.ppermute(prepare(*values), AXES, pairs)

        return self.plan.link(name, rank, cost, needs, run)


def same(value):
    return value


def gather_chunk(links, name, rank, send, rows, width):
    size = rows * width
    first = links.swap(name + "_x", rank, [send], same, size, BIT_HALF)
    second = links.swap(name + "_a", rank, [first], same, size, BIT_Y, BIT_Z)
    third = links.swap(name + "_b", rank, [first], same, size, BIT_Z, BIT_Y)
    fourth = links.swap(name + "_ab", rank, [second], same, size, BIT_Z, BIT_Y)
    pieces = []
    for near in (first, second, third, fourth):
        pieces.append(near)
        pieces.append(links.swap(near.name + "c", rank, [near], same, size, BIT_CORE))
    return pieces


def reduce_chunk(links, plan, name, rank, even, ready, count, rows, width, quarter):
    core = links.core
    p_bits = (BIT_Y, BIT_Z) if even else (BIT_Z, BIT_Y)
    q_bits = (p_bits[1], p_bits[0])
    at = {BIT_Y: links.y, BIT_Z: links.z}
    p = jnp.where(core == 0, at[p_bits[0]], at[p_bits[1]])
    q = jnp.where(core == 0, at[q_bits[0]], at[q_bits[1]])
    first = core == 0
    size = count * rows * width
    send_b = (1 - core, jnp.where(first, p, 1 - p))
    keep_a = (core, jnp.where(first, 1 - p, p))

    def core_task(step, cost, needs, run):
        return plan.core(name + step, rank, cost * (0.5 + 0.5 * count), needs, run)

    def swap(step, needs, prepare, size, *bits):
        return links.swap(name + step, rank, needs, prepare, size, *bits)

    cut = core_task("cut", 3.0, [ready], lambda v: (quarter(v, 1, 1 - p), quarter(v, *send_b)))
    got_a = swap("sa", [cut], lambda v: v[0], size, BIT_HALF, p_bits[1])
    got_b = swap("sb", [cut, got_a], lambda v, _: v[1], size, BIT_HALF, p_bits[1])
    sum_a = core_task("aa", 2.5, [ready, got_a], lambda v, g: add_low(quarter(v, *keep_a), g))
    got_c = swap("sc", [sum_a], same, size, p_bits[0], BIT_HALF)

    def add_three(v, g, h):
        total = add_low(quarter(v, 0, p), g, h).reshape(count, 2, rows // 2, width)
        return pick(total, 1 - q, 1), pick(total, q, 1)

    sum_b = core_task("ab", 3.5, [ready, got_b, got_c], add_three)
    got_d = swap("sd", [sum_b], lambda v: v[0], size // 2, *q_bits)
    total = core_task("ad", 1.5, [sum_b, got_d], lambda v, d: add_low(v[1], d))
    bit = BIT_REST
    while bit < links.devices:
        got = swap("se", [total], same, size // 2, bit)
        total = core_task("ae", 1.5, [total, got], add_low)
        bit *= 2
    at_q = swap("gq", [total], same, size // 2, *q_bits)
    at_p = swap("gp", [total], same, size // 2, *p_bits)
    at_pq = swap("gr", [at_q], same, size // 2, *p_bits)

    def join(a, b, c, d):
        full = jnp.zeros((count, 2, 2, rows // 2, width), BF16)
        for value, (i, j) in ((a, (p, q)), (b, (p, 1 - q)), (c, (1 - p, q)), (d, (1 - p, 1 - q))):
            zero = jnp.zeros((), jnp.int32)
            full = lax.dynamic_update_slice(full, value[:, None, None], (zero, i, j, zero, zero))
        return full.reshape(count, 2 * rows, width)

    own = core_task("j", 5.0, [total, at_q, at_p, at_pq], join)
    other = swap("gc", [own], same, 2 * size, BIT_CORE)
    return own, other


def local(devices, *arguments):
    (
        inputs,
        cotangent,
        seq_lengths,
        qkv_weight,
        out_weight,
        up_weight,
        down_weight,
        vector_params,
        qkv_momentum,
        out_momentum,
        up_momentum,
        down_momentum,
        vector_momentum,
        qkv_variance,
        out_variance,
        up_variance,
        down_variance,
        vector_variance,
    ) = arguments
    plan = Plan()
    links = Links(plan, devices)
    half, core = links.half, links.core
    core_flag = core.reshape(1)
    slot_count, width = inputs.shape
    half_rows = width // 2
    quarter_rows = width // 4
    down_t = down_weight.T

    def given(value):
        task = Task("given", "core", 0, 0.0, [], None)
        task.value = value
        task.end = 0.0
        return task

    high = jnp.where(core == 0, links.z, links.y)
    low = jnp.where(core == 0, links.y, links.z)
    block_at = core * 2 + high
    spot = jnp.stack([half, core, high, low]).astype(jnp.int32)

    def send_qkvo(qkv, out):
        start = low * quarter_rows
        rows = lax.dynamic_slice_in_dim(qkv, start, quarter_rows, 0)
        chosen = lax.dynamic_slice_in_dim(out, start, quarter_rows, 0)
        for number in range(3):
            option = rows[:, number * width : (number + 1) * width]
            chosen = jnp.where(block_at == number, option, chosen)
        return chosen.astype(BF16)

    def send_piece(own):
        return pick(own.reshape(8, quarter_rows, width), block_at * 2 + low)

    vector_low = plan.core(
        "v_low", 0, 1.0, [given(vector_params)], lambda v: v.astype(BF16).reshape(6, width)
    )
    vector_other = links.swap("v", 0, [vector_low], same, 6 * width, BIT_HALF)
    sent_qkvo = plan.core("q_cut", 1, 8.0, [given(qkv_weight), given(out_weight)], send_qkvo)
    own_up = plan.core(
        "u_own", 2, 14.2, [given(up_weight)], lambda w: column_blocks([w], [4], 80)
    )
    sent_up = plan.core("u_cut", 2, 4.0, [own_up], send_piece)
    own_down = plan.core(
        "d_own", 3.5, 14.2, [given(down_t)], lambda w: column_blocks([w], [2], 160)
    )
    sent_down = plan.core("d_cut", 3.5, 2.5, [own_down], send_piece)
    own_qkvo = plan.core(
        "q_own",
        3,
        13.0,
        [given(qkv_weight), given(out_weight)],
        lambda w, o: column_blocks([w, o], [3, 1], 80),
    )
    pieces_qkvo = gather_chunk(links, "q_g", 1, sent_qkvo, quarter_rows, width)
    pieces_up = gather_chunk(links, "u_g", 2, sent_up, quarter_rows, width)
    pieces_down = gather_chunk(links, "d_g", 3, sent_down, quarter_rows, width)
    needs_qkvo = [own_qkvo] + pieces_qkvo
    needs_up = [own_up] + pieces_up
    needs_down = [own_down] + pieces_down

    def weights_of(by_rows, values):
        return Weights(by_rows, spot, values[0], values[1:])

    def prepare(lengths, grads):
        segment = layout(lengths[0], slot_count, BLK)
        position = jnp.arange(slot_count, dtype=jnp.int32)
        allowed = (segment[:, None] == segment[None, :]) & (position[None, :] <= position[:, None])
        fill = jnp.where(allowed, 0.0, NEG_FILL)
        live = (segment >= 0).astype(F32)[None, :]
        grad_low, grad_sum = mask_grad(grads, live)
        return fill, live, grad_low, grad_sum[0]

    prepared = plan.core("prepare", 7, 5.0, [given(seq_lengths), given(cotangent.T)], prepare)

    def join_vector(own, other):
        lower = half == 0
        pair = [jnp.where(lower, own, other), jnp.where(lower, other, own)]
        return jnp.concatenate(pair).astype(F32)

    vector = plan.core("v_join", 8, 1.0, [vector_low, vector_other], join_vector)
    normed = plan.core(
        "norm_one",
        9,
        4.0,
        [given(inputs.T), vector],
        lambda rows, vec: norm_one(rows, vec[0:1], vec[1:2]),
    )

    def qkv_bias(vec):
        return jnp.stack([vec[2], jnp.zeros_like(vec[2]), vec[3]])[:, None, :]

    projected = plan.core(
        "project",
        10,
        15.5,
        [normed, vector] + needs_qkvo,
        lambda n, vec, *w: project(n[0], weights_of(True, w), qkv_bias(vec)),
    )
    attended = plan.core(
        "attend", 11, 19.0, [projected, prepared], lambda qkv, prep: attend_forward(qkv, prep[0])
    )
    residual = plan.core(
        "out",
        12,
        12.0,
        [attended, normed, vector] + needs_qkvo,
        lambda att, n, vec, *w: out_and_norm(
            att[0], weights_of(True, w), n[1], vec[4:5], vec[5:6], vec[6:7]
        ),
    )
    activated = plan.core(
        "up",
        16,
        24.0,
        [residual, vector] + needs_up,
        lambda res, vec, *w: up_and_gelu(res[1], weights_of(True, w), vec[7:11][:, None, :]),
    )

    def places(*entries):
        return jnp.stack([jnp.asarray(entry, jnp.int32) for entry in entries])

    def down_product(act, prep, at_core, got=None):
        at = places(0, 2 * (1 - half) + at_core, 0, 2 * half + at_core)
        return outer_products(prep[2][None], act[0], at, got)

    block_size = width * width
    down_sent = plan.core(
        "d_s", 20, 12.5, [activated, prepared], lambda a, p: down_product(a, p, 1 - core)
    )
    down_got = links.swap("d_c", 20, [down_sent], same, 2 * block_size, BIT_CORE)
    down_kept = plan.core(
        "d_k",
        22,
        17.0,
        [activated, prepared, down_got],
        lambda a, p, got: down_product(a, p, core, got),
    )

    def cut_piece(value, lead, sizes):
        start = [jnp.asarray(at, jnp.int32) for at in lead] + [jnp.zeros((), jnp.int32)] * 2
        piece = lax.dynamic_slice(value, start, sizes + (quarter_rows, width))
        return piece.reshape(-1, quarter_rows, width)

    def down_quarter(value, away, p):
        value = value.reshape(2, 2, 2, quarter_rows, width)
        return cut_piece(value, (1 - away, 0, p), (1, 2, 1))

    def up_quarter(value, away, p):
        value = value.reshape(2, 2, 2, quarter_rows, width)
        return cut_piece(value, (0, half ^ away, p), (2, 1, 1))

    def block_quarter(value, away, p):
        value = value.reshape(2, 2, quarter_rows, width)
        return cut_piece(value, (half ^ away, p), (1, 1))

    def reduce(name, rank, even, ready, count, quarter):
        return reduce_chunk(
            links, plan, name, rank, even, ready, count, quarter_rows, width, quarter
        )

    down_sum = reduce("d", 0.1, True, down_kept, 2, down_quarter)

    grad_pre = plan.core(
        "g_pre",
        30,
        24.0,
        [prepared, activated] + needs_down,
        lambda prep, act, *w: grad_pre_act(prep[2], weights_of(False, w), act[1]),
    )
    def up_product(res, g, at_core, got=None):
        return outer_products(res[1][None], g[0], places(0, at_core, 0, 2 + at_core), got)

    up_sent = plan.core("u_s", 31, 12.5, [residual, grad_pre], lambda r, g: up_product(r, g, 1 - core))
    up_got = links.swap("u_c", 31, [up_sent], same, 2 * block_size, BIT_CORE)
    branch = plan.core(
        "n2_b",
        32,
        28.0,
        [grad_pre, residual, prepared, vector] + needs_up,
        lambda g, res, prep, vec, *w: norm_two_back(
            g[0], weights_of(True, w), res[0], prep[2], vec[5:6]
        ),
    )
    up_kept = plan.core(
        "u_k",
        33,
        17.0,
        [residual, grad_pre, up_got],
        lambda r, g, got: up_product(r, g, core, got),
    )
    up_sum = reduce("u", 0.2, False, up_kept, 2, up_quarter)

    grad_attended = plan.core(
        "g_att",
        34,
        9.0,
        [branch] + needs_qkvo,
        lambda b, *w: grad_attended_of(b[1], weights_of(True, w)),
    )
    pairs = pl.cdiv(width, 2 * HD)
    early = pairs // 2
    back_needs = [projected, grad_attended, prepared, attended]
    grad_early = plan.core(
        "att_b",
        35,
        16.0,
        back_needs,
        lambda qkv, g, prep, att: attend_backward(qkv, g, prep[0], att[1], 0, early),
    )
    grad_parts = plan.core(
        "att_b",
        35,
        17.0,
        back_needs + [grad_early],
        lambda qkv, g, prep, att, some: attend_backward(
            qkv, g, prep[0], att[1], early, pairs - early, some
        ),
    )

    def first_product(n, att, b, parts, at_core, got=None):
        left = jnp.where(at_core == 0, n[0], att[0])
        right = jnp.where(at_core == 0, parts[0], b[1])
        return outer_products(left[None], right[None], places(0, 0), got)

    def second_product(n, att, b, parts, at_core, got=None):
        return outer_products(n[0][None], parts, places(0, 1 + at_core), got)

    attention_needs = [normed, attended, branch, grad_parts]
    attention_sums = []
    for number, product in enumerate((first_product, second_product)):
        name = "ab"[number]
        sent = plan.core(
            name + "_s",
            36 + number,
            7.5,
            attention_needs,
            lambda *v, product=product: product(*v, 1 - core),
        )
        got = links.swap(name + "_c", 36 + number, [sent], same, block_size, BIT_CORE)
        kept = plan.core(
            name + "_k",
            38 + number,
            9.0,
            attention_needs + [got],
            lambda *v, product=product: product(*v[:4], core, v[4]),
        )
        attention_sums.append(
            reduce(name, 0.3 + 0.1 * number, number == 0, kept, 1, block_quarter)
        )
    grad_input = plan.core(
        "n1_b",
        38,
        21.5,
        [grad_parts, normed, branch, vector] + needs_qkvo,
        lambda parts, n, b, vec, *w: norm_one_back(
            parts, weights_of(True, w), n[1], b[0], vec[0:1]
        ),
    )

    def vector_grads(parts, b, g, grad_in, prep):
        part_sums = jnp.sum(parts.astype(F32), axis=1)
        rows = [grad_in[1][0], grad_in[1][1], part_sums[0], part_sums[2]]
        rows += [b[2][2], b[2][0], b[2][1]]
        rows += [g[1][j, 0] for j in range(4)] + [prep[3]]
        both = jnp.stack(rows).reshape(2, 6, width)
        return pick(both, 1 - half), pick(both, half)

    vector_grad = plan.core(
        "v_grad", 39, 3.0, [grad_parts, branch, grad_pre, grad_input, prepared], vector_grads
    )
    vector_got = links.swap("v_x", 39, [vector_grad], lambda v: v[0], 12 * width, BIT_HALF)
    vector_sum = plan.core(
        "v_add", 39, 0.5, [vector_grad, vector_got], lambda v, g: v[1] + g
    )
    bit = BIT_CORE
    while bit < devices:
        vector_got = links.swap("v_dp", 39, [vector_sum], same, 12 * width, bit)
        vector_sum = plan.core("v_add", 39, 0.5, [vector_sum, vector_got], jnp.add)
        bit *= 2

    layer = plan.core(
        "layer",
        40,
        22.0,
        [activated, residual, prepared, vector] + needs_down,
        lambda act, res, prep, vec, *w: layer_out(
            act[0], weights_of(False, w), res[0], prep[1], vec[11:12]
        ),
    )

    up_state = (up_weight, up_momentum, up_variance)
    down_state = (down_t, down_momentum.T, down_variance.T)
    qkv_state = (qkv_weight, qkv_momentum, qkv_variance)
    out_state = (out_weight, out_momentum, out_variance)

    def update(name, rank, cost, state, sums, earlier, run):
        needs = [task for pair in sums for task in pair] + ([earlier] if earlier else [])

        def call(*v):
            pairs = [v[2 * i : 2 * i + 2] for i in range(len(sums))]
            picks, extra = run(pairs)
            return adamw_part(core_flag, state, picks, 80, earlier=v[-1] if earlier else None, **extra)

        return plan.core(name, rank, cost, needs, call)

    new_down = new_up = None
    for part in range(2):
        new_down = update(
            "n_d",
            50,
            28.0,
            down_state,
            [down_sum],
            new_down,
            lambda pairs, part=part: (
                [(pairs[0], part, 0), (pairs[0], part, 1)],
                dict(row_part=part),
            ),
        )
    for part in range(2):
        new_up = update(
            "n_u",
            52,
            28.5,
            up_state,
            [up_sum],
            new_up,
            lambda pairs, part=part: (
                [(pairs[0], part, 0), (pairs[0], part, 1)],
                dict(col_part=part),
            ),
        )
    new_out = update(
        "n_o", 54, 15.0, out_state, attention_sums[:1], None, lambda p: ([(p[0], 0, 1)], {})
    )
    new_qkv = update(
        "n_q",
        55,
        39.0,
        qkv_state,
        attention_sums,
        None,
        lambda p: ([(p[0], 0, 0), (p[1], 0, 0), (p[1], 0, 1)], {}),
    )
    new_vector = plan.core(
        "n_v",
        45,
        1.0,
        [vector_sum],
        lambda g: adamw_step(
            vector_params, g.reshape(-1), vector_momentum, vector_variance, 0.0, VECTOR_RATE
        ),
    )
    plan.trace()
    states = [
        (new_qkv.value[i], new_out.value[i], new_up.value[i], new_down.value[i].T, new_vector.value[i])
        for i in range(3)
    ]
    return (layer.value.T, grad_input.value[0].T) + states[0] + states[1] + states[2]


def solution(mesh):
    rows = P(("dp", "shard"), None)
    halves = P("shard", None)
    vector = P("shard")
    state = (halves, halves, halves, halves, vector)
    return jax.shard_map(
        functools.partial(local, mesh.shape["dp"] * mesh.shape["shard"]),
        mesh=mesh,
        in_specs=(rows, rows, rows) + state * 3,
        out_specs=(rows, rows) + state * 3,
        check_vma=False,
    )
```
